32 devices in a mesh: expert: 16 (over z, y, core), hidden: 2 (over x).
Axes of the slice: x: 2, y: 2, z: 4, core: 2. Of those that a mesh axis runs over, the one named last changes fastest.
Arguments:
- tokens: bfloat16 [4096, 2048], P('expert'), may hold values from -6 to 6
- gates: float32 [4096, 2], P('expert'), may hold values from 0.2 to 1
- routes: int32 [4096, 2], P('expert'), may hold values from 0 to 15, all different within a row; in each aligned block of 256 rows (0 to 255, 256 to 511, ...) at most 48 rows name the same one
- w_up: bfloat16 [16, 2048, 4096], P('expert', None, 'hidden'), may hold values from -0.125 to 0.125
- w_down: bfloat16 [16, 4096, 2048], P('expert', 'hidden'), may hold values from -0.09375 to 0.09375
- cotangent: bfloat16 [4096, 2048], P('expert', 'hidden'), may hold values from -6 to 6
Outputs:
- mixed: bfloat16 [4096, 2048], P('expert', 'hidden')
- grad_tokens: bfloat16 [4096, 2048], P('expert', 'hidden')
- grad_up: bfloat16 [16, 2048, 4096], P('expert', None, 'hidden')
- grad_down: bfloat16 [16, 4096, 2048], P('expert', 'hidden')
The draws below stay inside these ranges and needn't reach their ends.
Inputs may be any that keep to these rules, and one draw needn't show every extreme that they name: `routes`: each row names 2 different experts. Within each aligned block of 256 rows no expert is named by more than 48 rows, a bound that some block reaches.
All inputs are finite; a program needn't handle non-finite values.
Results may differ from the reference program's by a relative error of at most 0.009.
Values may be sent and summed in bfloat16 or wider, within the bound.
A program may use at most 128 MiB of HBM per device.

```python
import math
import jax
import jax.numpy as jnp
import numpy as np
from jax import lax

D = 2048
FF = 4096
TOP = 2
TOK_DEV = 256
EXPERTS = 16
CAP_SRC = 48
TOKENS = 4096
N_HIDDEN = 2


def steps_of(rng, extent, split, smallest, top_value):
    def one(dim, parts):
        draws = jax.random.uniform(jax.random.fold_in(jax.random.fold_in(rng, 6), dim), (parts,), jnp.float32, smallest / len(split), top_value / len(split))
        return jnp.repeat(jnp.exp(draws), extent[dim] // parts).reshape((-1,) + (1,) * (len(extent) - dim - 1))

    loudness = one(*split[0])
    for cut in split[1:]:
        loudness = loudness * one(*cut)
    return loudness


def assign_block(rng, own, number, rows, amount, top, reach, lean):
    sequence = jax.random.permutation(rng, amount)
    crowded, ordinary = portions_of(amount, rows * top, reach, lean, True), portions_of(amount, rows * top, reach, lean, False)
    places = jnp.arange(amount)

    def named(sizes, rotation):
        used = int((sizes > 0).sum())
        fixed = max(1, used // 4)
        passed = fixed + (places - fixed + rotation * (used - fixed)) % max(1, amount - fixed)
        return jnp.zeros((amount,), jnp.int32).at[sequence[jnp.where(places < fixed, places, passed)]].set(jnp.asarray(sizes, jnp.int32))

    sizes = jnp.where(number % 4 == 0, named(crowded, number // 4), named(ordinary, number - number // 4 - 1))
    mixed = jax.random.permutation(jax.random.fold_in(own, 3), amount)
    giver, receiver = mixed[0:amount // 2 * 2:2], mixed[1:amount // 2 * 2:2]
    margin = jnp.minimum(sizes[giver] - 1, reach - sizes[receiver]) // 2
    margin = jnp.where((giver == sequence[0]) | (receiver == sequence[0]) | (sizes[receiver] == 0), 0, jnp.maximum(margin, 0))
    passed = jax.random.randint(jax.random.fold_in(own, 4), (amount // 2,), 0, 1 << 20) % (margin + 1)
    sizes = sizes.at[giver].add(-passed).at[receiver].add(passed)
    items = jnp.searchsorted(jnp.cumsum(sizes), jnp.arange(rows * top), side="right").astype(jnp.int32)
    listing = items.reshape(top, rows).T
    listing = listing[jax.random.permutation(jax.random.fold_in(own, 1), rows)]
    rotation = jax.random.randint(jax.random.fold_in(own, 2), (rows, 1), 0, top)
    return jnp.take_along_axis(listing, (jnp.arange(top)[None, :] + rotation) % top, axis=1)


def portions_of(amount, total, bound, slope, full):
    loads = [(1 << 20) // math.isqrt(rank ** slope) + 1 for rank in range(1, amount + 1)]
    largest = bound if full else min(bound, max(-(-total // amount), total * loads[0] // sum(loads)))
    least = 1 if total - largest >= amount - 1 else 0
    counts, spare = [largest] + [least] * (amount - 1), total - largest - least * (amount - 1)
    while spare > 0:
        movable = [i for i in range(1, amount) if counts[i] < largest] or [i for i in range(1, amount) if counts[i] < bound]
        pool, budget = sum([loads[i] for i in movable]), spare
        for i in movable:
            more = min(bound - counts[i], max(1, budget * loads[i] // pool), spare)
            counts[i] = counts[i] + more
            spare = spare - more
    return np.array(counts)


def noise(stream_key, dims, scale, reach, cuts=(), kind=jnp.bfloat16):
    factor_of = steps_of(stream_key, dims, cuts, -0.22, 0.18) if cuts else 1.0
    result = jax.random.normal(stream_key, dims, jnp.float32) * scale * factor_of
    return jnp.minimum(jnp.maximum(result, -reach), reach).astype(kind)


def setup_inputs(seed: int = 0) -> dict:
    streams_of = jax.random.split(jax.random.key(seed), 7)
    tokens = noise(streams_of[0], (TOKENS, D), 1.0, 6.0, ((0, 16),))
    gates = jnp.clip(0.2 + 0.8 * jax.random.uniform(streams_of[1], (TOKENS, TOP), jnp.float32) ** steps_of(streams_of[1], (TOKENS, TOP), ((0, 16),), -0.2, 0.2), 0.2, 1.0)
    routes_keys = jax.random.split(jax.random.fold_in(streams_of[2], 1), TOKENS // TOK_DEV)
    routes_turns = jax.random.permutation(jax.random.fold_in(streams_of[2], 3), TOKENS // TOK_DEV)
    routes = jax.vmap(lambda own, number: assign_block(jax.random.fold_in(streams_of[2], 2), own, number, TOK_DEV, EXPERTS, TOP, CAP_SRC, 1))(routes_keys, routes_turns).reshape((TOKENS, TOP))
    w_up = noise(streams_of[3], (EXPERTS, D, FF), D ** -0.5, 0.125, ((0, 16), (2, 2)))
    w_down = noise(streams_of[4], (EXPERTS, FF, D), FF ** -0.5, 0.09375, ((0, 16), (1, 2)))
    cotangent = noise(streams_of[5], (TOKENS, D), 1.0, 6.0, ((0, 16), (1, 2)))
    return dict(tokens=tokens, gates=gates, routes=routes, w_up=w_up, w_down=w_down, cotangent=cotangent)


def gelu_fn(values):
    return jax.nn.gelu(values, approximate=True)

def reference(tokens, gates, routes, w_up, w_down, cotangent):
    blocks = TOKENS // TOK_DEV
    slot_rows = blocks * CAP_SRC
    shard_units = FF // N_HIDDEN
    flat_routes = routes.reshape(blocks, TOK_DEV * TOP)
    member = (flat_routes[:, :, None] == jnp.arange(EXPERTS, dtype=jnp.int32)[None, None, :]).astype(jnp.int32)
    before = jnp.cumsum(member, axis=1) - member
    slot_place = lax.optimization_barrier(jnp.sum(before * member, axis=2))
    position = (jnp.arange(blocks, dtype=jnp.int32)[:, None] * CAP_SRC + slot_place).reshape(TOKENS, TOP).astype(jnp.int32)
    expert_in = jnp.zeros((EXPERTS, slot_rows, D), jnp.bfloat16)
    grad_out = jnp.zeros((EXPERTS, slot_rows, D), jnp.bfloat16)
    cot_float = cotangent.astype(jnp.float32)
    for which in range(TOP):
        expert_in = expert_in.at[routes[:, which], position[:, which]].set(tokens)
        gated = (gates[:, which:which + 1] * cot_float).astype(jnp.bfloat16)
        grad_out = grad_out.at[routes[:, which], position[:, which]].set(gated)

    def one_expert(operands):
        expert_in_e, grad_out_e, up_mat, down_mat = operands
        pre_act = jnp.dot(expert_in_e, up_mat, preferred_element_type=jnp.float32)
        activated, gelu_back = jax.vjp(gelu_fn, pre_act)
        hidden_act = activated.astype(jnp.bfloat16)
        act_split = hidden_act.reshape(slot_rows, N_HIDDEN, shard_units).astype(jnp.float32)
        down_split = down_mat.reshape(N_HIDDEN, shard_units, D).astype(jnp.float32)
        partial_value = jnp.einsum('rhf,hfd->hrd', act_split, down_split)
        partial_value = lax.optimization_barrier(partial_value.astype(jnp.bfloat16))
        out_sum = lax.optimization_barrier(jnp.sum(partial_value.astype(jnp.float32), axis=0))
        grad_hidden = jnp.dot(grad_out_e, down_mat.T, preferred_element_type=jnp.float32)
        grad_pre = gelu_back(grad_hidden)[0].astype(jnp.bfloat16)
        grad_down_e = jnp.dot(hidden_act.T, grad_out_e, preferred_element_type=jnp.float32).astype(jnp.bfloat16)
        grad_up_e = jnp.dot(expert_in_e.T, grad_pre, preferred_element_type=jnp.float32).astype(jnp.bfloat16)
        grad_split = grad_pre.reshape(slot_rows, N_HIDDEN, shard_units).astype(jnp.float32)
        up_split = up_mat.reshape(D, N_HIDDEN, shard_units).astype(jnp.float32)
        input_terms = jnp.einsum('rhf,dhf->hrd', grad_split, up_split)
        input_terms = lax.optimization_barrier(input_terms.astype(jnp.bfloat16))
        input_sum = lax.optimization_barrier(jnp.sum(input_terms.astype(jnp.float32), axis=0))
        return (out_sum, input_sum, grad_up_e, grad_down_e)
    out_sum, input_sum, grad_up, grad_down = lax.map(one_expert, (expert_in, grad_out, w_up, w_down))
    mixed = jnp.zeros((TOKENS, D), jnp.float32)
    grad_tokens = jnp.zeros((TOKENS, D), jnp.float32)
    for which in range(TOP):
        mixed = mixed + gates[:, which:which + 1] * out_sum[routes[:, which], position[:, which]]
        grad_tokens = grad_tokens + input_sum[routes[:, which], position[:, which]]
    return (mixed.astype(jnp.bfloat16), grad_tokens.astype(jnp.bfloat16), grad_up, grad_down)
```

```python
import jax
import jax.numpy as jnp
from jax import lax
from jax.sharding import PartitionSpec as P

CHUNKS = 1


def gelu_fn(values):
    return jax.nn.gelu(values, approximate=True)


def swap(block):
    return lax.ppermute(block, "hidden", [(0, 1), (1, 0)])


def gather_features(block):
    if lax.axis_size("hidden") != 2:
        return lax.all_gather(block, "hidden", axis=1, tiled=True)
    other = swap(block)
    first = lax.axis_index("hidden") == 0
    return jnp.concatenate(
        [jnp.where(first, block, other), jnp.where(first, other, block)], axis=1
    )


def summed_features(rows, weight, contract):
    def product(part):
        return lax.dot_general(
            rows, part, (((1,), (contract,)), ((), ())), preferred_element_type=jnp.float32
        ).astype(jnp.bfloat16)

    if lax.axis_size("hidden") != 2:
        return lax.psum_scatter(product(weight), "hidden", scatter_dimension=1, tiled=True)
    axis = 1 - contract
    width = weight.shape[axis] // 2
    me = lax.axis_index("hidden")
    moving = swap(product(lax.dynamic_slice_in_dim(weight, (1 - me) * width, width, axis)))
    kept = product(lax.dynamic_slice_in_dim(weight, me * width, width, axis))
    return (kept.astype(jnp.float32) + moving.astype(jnp.float32)).astype(jnp.bfloat16)


def exchange(block):
    return lax.all_to_all(block, "expert", split_axis=0, concat_axis=0, tiled=True)


def per_device(tokens, gates, routes, w_up, w_down, cotangent):
    expert_count = lax.axis_size("expert")
    tok_rows, top_count = routes.shape
    capacity = 3 * tok_rows * top_count // (2 * expert_count)
    depth = capacity // CHUNKS
    flat_routes = routes.reshape(-1)
    member = (flat_routes[:, None] == jnp.arange(expert_count, dtype=jnp.int32)[None, :]).astype(
        jnp.bfloat16
    )
    order = jnp.arange(tok_rows * top_count, dtype=jnp.int32)
    earlier = (order[:, None] > order[None, :]).astype(jnp.bfloat16)
    before = jnp.dot(earlier, member, preferred_element_type=jnp.float32)
    slot_place = jnp.sum(before * member.astype(jnp.float32), axis=1).astype(jnp.int32)
    slot_chunk = slot_place // depth
    target = (flat_routes * depth + slot_place % depth).reshape(tok_rows, top_count)
    slot_chunk = slot_chunk.reshape(tok_rows, top_count)
    slot_ids = jnp.arange(expert_count * depth, dtype=jnp.int32)

    def selector(chunk, which):
        aim = jnp.where(slot_chunk[:, which] == chunk, target[:, which], -1)
        return (aim[None, :] == slot_ids[:, None]).astype(jnp.bfloat16)

    picks = [[selector(chunk, which) for which in range(top_count)] for chunk in range(CHUNKS)]
    up_local = w_up[0]
    down_local = w_down[0]
    width = cotangent.shape[1]
    own_tokens = lax.dynamic_slice_in_dim(tokens, lax.axis_index("hidden") * width, width, 1)
    cot_float = cotangent.astype(jnp.float32)
    gated = jnp.concatenate(
        [(gates[:, k : k + 1] * cot_float).astype(jnp.bfloat16) for k in range(top_count)], axis=0
    )
    got_tokens = [
        exchange(
            jnp.dot(sum(pick[1:], pick[0]), own_tokens, preferred_element_type=jnp.float32).astype(
                jnp.bfloat16
            )
        )
        for pick in picks
    ]
    got_grads = [
        exchange(
            jnp.dot(
                jnp.concatenate(pick, axis=1), gated, preferred_element_type=jnp.float32
            ).astype(jnp.bfloat16)
        )
        for pick in picks
    ]
    hidden_acts, backs, expert_ins, grad_outs, grad_pres = [], [], [], [], []
    returned, input_back = [], []
    for got in got_tokens:
        expert_in = gather_features(got)
        pre_act = jnp.dot(expert_in, up_local, preferred_element_type=jnp.float32)
        activated, gelu_back = jax.vjp(gelu_fn, pre_act)
        hidden_act = activated.astype(jnp.bfloat16)
        returned.append(exchange(summed_features(hidden_act, down_local, 0)))
        expert_ins.append(expert_in)
        hidden_acts.append(hidden_act)
        backs.append(gelu_back)
    for got, gelu_back in zip(got_grads, backs):
        grad_out = gather_features(got)
        grad_hidden = lax.dot_general(
            grad_out, down_local, (((1,), (1,)), ((), ())), preferred_element_type=jnp.float32
        )
        grad_pre = gelu_back(grad_hidden)[0].astype(jnp.bfloat16)
        input_back.append(exchange(summed_features(grad_pre, up_local, 1)))
        grad_outs.append(grad_out)
        grad_pres.append(grad_pre)

    def outer(left, right):
        return lax.dot_general(
            jnp.concatenate(left, axis=0),
            jnp.concatenate(right, axis=0),
            (((0,), (0,)), ((), ())),
            preferred_element_type=jnp.float32,
        ).astype(jnp.bfloat16)

    grad_down = outer(hidden_acts, grad_outs)
    grad_up = outer(expert_ins, grad_pres)

    def picked(which, arrays):
        total = None
        for pick, array in zip(picks, arrays):
            part = lax.dot_general(
                pick[which], array, (((0,), (0,)), ((), ())), preferred_element_type=jnp.float32
            )
            total = part if total is None else total + part
        return total

    mixed = sum(gates[:, k : k + 1] * picked(k, returned) for k in range(top_count))
    grad_tokens = sum(picked(k, input_back) for k in range(top_count))
    return (
        mixed.astype(jnp.bfloat16),
        grad_tokens.astype(jnp.bfloat16),
        grad_up[None],
        grad_down[None],
    )


def solution(mesh):
    placed = (
        P("expert", None),
        P("expert", None),
        P("expert", None),
        P("expert", None, "hidden"),
        P("expert", "hidden", None),
        P("expert", "hidden"),
    )
    return jax.shard_map(
        per_device,
        mesh=mesh,
        in_specs=placed,
        out_specs=(
            P("expert", "hidden"),
            P("expert", "hidden"),
            P("expert", None, "hidden"),
            P("expert", "hidden", None),
        ),
        check_vma=False,
    )
```

```python
import jax
import jax.numpy as jnp
from jax import lax
from jax.sharding import PartitionSpec as P

CHUNKS = 1


def gelu_fn(values):
    return jax.nn.gelu(values, approximate=True)


def swap(block):
    return lax.ppermute(block, "hidden", [(0, 1), (1, 0)])


def gather_features(block):
    if lax.axis_size("hidden") != 2:
        return lax.all_gather(block, "hidden", axis=1, tiled=True)
    other = swap(block)
    first = lax.axis_index("hidden") == 0
    return jnp.concatenate(
        [jnp.where(first, block, other), jnp.where(first, other, block)], axis=1
    )


def summed_features(rows, weight, contract):
    def product(part):
        return lax.dot_general(
            rows, part, (((1,), (contract,)), ((), ())), preferred_element_type=jnp.float32
        ).astype(jnp.bfloat16)

    if lax.axis_size("hidden") != 2:
        return lax.psum_scatter(product(weight), "hidden", scatter_dimension=1, tiled=True)
    axis = 1 - contract
    width = weight.shape[axis] // 2
    me = lax.axis_index("hidden")
    moving = swap(product(lax.dynamic_slice_in_dim(weight, (1 - me) * width, width, axis)))
    kept = product(lax.dynamic_slice_in_dim(weight, me * width, width, axis))
    return (kept.astype(jnp.float32) + moving.astype(jnp.float32)).astype(jnp.bfloat16)


def sent_outputs(rows, weight):
    if lax.axis_size("hidden") != 2:
        return summed_features(rows, weight, 0)
    return jnp.dot(rows, weight, preferred_element_type=jnp.float32).astype(jnp.bfloat16)


def summed_mixed(mixed):
    if lax.axis_size("hidden") != 2:
        return mixed
    width = mixed.shape[1] // 2
    first = lax.axis_index("hidden") == 0
    low, high = mixed[:, :width], mixed[:, width:]
    moving = swap(jnp.where(first, high, low).astype(jnp.bfloat16))
    return jnp.where(first, low, high) + moving.astype(jnp.float32)


def exchange(block):
    return lax.all_to_all(block, "expert", split_axis=0, concat_axis=0, tiled=True)


def per_device(tokens, gates, routes, w_up, w_down, cotangent):
    expert_count = lax.axis_size("expert")
    tok_rows, top_count = routes.shape
    capacity = 3 * tok_rows * top_count // (2 * expert_count)
    depth = capacity // CHUNKS
    flat_routes = routes.reshape(-1)
    member = (flat_routes[:, None] == jnp.arange(expert_count, dtype=jnp.int32)[None, :]).astype(
        jnp.bfloat16
    )
    order = jnp.arange(tok_rows * top_count, dtype=jnp.int32)
    earlier = (order[:, None] > order[None, :]).astype(jnp.bfloat16)
    before = jnp.dot(earlier, member, preferred_element_type=jnp.float32)
    slot_place = jnp.sum(before * member.astype(jnp.float32), axis=1).astype(jnp.int32)
    slot_chunk = slot_place // depth
    target = (flat_routes * depth + slot_place % depth).reshape(tok_rows, top_count)
    slot_chunk = slot_chunk.reshape(tok_rows, top_count)
    slot_ids = jnp.arange(expert_count * depth, dtype=jnp.int32)

    def selector(chunk, which):
        aim = jnp.where(slot_chunk[:, which] == chunk, target[:, which], -1)
        return (aim[None, :] == slot_ids[:, None]).astype(jnp.bfloat16)

    picks = [[selector(chunk, which) for which in range(top_count)] for chunk in range(CHUNKS)]
    up_local = w_up[0]
    down_local = w_down[0]
    width = cotangent.shape[1]
    own_tokens = lax.dynamic_slice_in_dim(tokens, lax.axis_index("hidden") * width, width, 1)
    cot_float = cotangent.astype(jnp.float32)
    gated = jnp.concatenate(
        [(gates[:, k : k + 1] * cot_float).astype(jnp.bfloat16) for k in range(top_count)], axis=0
    )
    got_tokens = [
        exchange(
            jnp.dot(sum(pick[1:], pick[0]), own_tokens, preferred_element_type=jnp.float32).astype(
                jnp.bfloat16
            )
        )
        for pick in picks
    ]
    got_grads = [
        exchange(
            jnp.dot(
                jnp.concatenate(pick, axis=1), gated, preferred_element_type=jnp.float32
            ).astype(jnp.bfloat16)
        )
        for pick in picks
    ]
    hidden_acts, backs, expert_ins, grad_outs, grad_pres = [], [], [], [], []
    returned, input_back = [], []
    for got in got_tokens:
        expert_in = gather_features(got)
        pre_act = jnp.dot(expert_in, up_local, preferred_element_type=jnp.float32)
        activated, gelu_back = jax.vjp(gelu_fn, pre_act)
        hidden_act = activated.astype(jnp.bfloat16)
        returned.append(exchange(sent_outputs(hidden_act, down_local)))
        expert_ins.append(expert_in)
        hidden_acts.append(hidden_act)
        backs.append(gelu_back)
    for got, gelu_back in zip(got_grads, backs):
        grad_out = gather_features(got)
        grad_hidden = lax.dot_general(
            grad_out, down_local, (((1,), (1,)), ((), ())), preferred_element_type=jnp.float32
        )
        grad_pre = gelu_back(grad_hidden)[0].astype(jnp.bfloat16)
        input_back.append(exchange(summed_features(grad_pre, up_local, 1)))
        grad_outs.append(grad_out)
        grad_pres.append(grad_pre)

    def outer(left, right):
        return lax.dot_general(
            jnp.concatenate(left, axis=0),
            jnp.concatenate(right, axis=0),
            (((0,), (0,)), ((), ())),
            preferred_element_type=jnp.float32,
        ).astype(jnp.bfloat16)

    grad_down = outer(hidden_acts, grad_outs)
    grad_up = outer(expert_ins, grad_pres)

    def picked(which, arrays):
        total = None
        for pick, array in zip(picks, arrays):
            part = lax.dot_general(
                pick[which], array, (((0,), (0,)), ((), ())), preferred_element_type=jnp.float32
            )
            total = part if total is None else total + part
        return total

    mixed = sum(gates[:, k : k + 1] * picked(k, returned) for k in range(top_count))
    grad_tokens = sum(picked(k, input_back) for k in range(top_count))
    return (
        summed_mixed(mixed).astype(jnp.bfloat16),
        grad_tokens.astype(jnp.bfloat16),
        grad_up[None],
        grad_down[None],
    )


def solution(mesh):
    placed = (
        P("expert", None),
        P("expert", None),
        P("expert", None),
        P("expert", None, "hidden"),
        P("expert", "hidden", None),
        P("expert", "hidden"),
    )
    return jax.shard_map(
        per_device,
        mesh=mesh,
        in_specs=placed,
        out_specs=(
            P("expert", "hidden"),
            P("expert", "hidden"),
            P("expert", None, "hidden"),
            P("expert", "hidden", None),
        ),
        check_vma=False,
    )
```

```python
import jax
import jax.numpy as jnp
from jax import lax
from jax.sharding import PartitionSpec as P

CHUNKS = 1


def gelu_fn(values):
    return jax.nn.gelu(values, approximate=True)


def swap(block):
    return lax.ppermute(block, "hidden", [(0, 1), (1, 0)])


def gather_features(block):
    if lax.axis_size("hidden") != 2:
        return lax.all_gather(block, "hidden", axis=1, tiled=True)
    other = swap(block)
    first = lax.axis_index("hidden") == 0
    return jnp.concatenate(
        [jnp.where(first, block, other), jnp.where(first, other, block)], axis=1
    )


def summed_features(rows, weight, contract):
    def product(part):
        return lax.dot_general(
            rows, part, (((1,), (contract,)), ((), ())), preferred_element_type=jnp.float32
        ).astype(jnp.bfloat16)

    if lax.axis_size("hidden") != 2:
        return lax.psum_scatter(product(weight), "hidden", scatter_dimension=1, tiled=True)
    axis = 1 - contract
    width = weight.shape[axis] // 2
    me = lax.axis_index("hidden")
    moving = swap(product(lax.dynamic_slice_in_dim(weight, (1 - me) * width, width, axis)))
    kept = lax.optimization_barrier(
        product(lax.dynamic_slice_in_dim(weight, me * width, width, axis))
    )
    return (kept.astype(jnp.float32) + moving.astype(jnp.float32)).astype(jnp.bfloat16)


def sent_outputs(rows, weight):
    if lax.axis_size("hidden") != 2:
        return summed_features(rows, weight, 0)
    return jnp.dot(rows, weight, preferred_element_type=jnp.float32).astype(jnp.bfloat16)


def summed_mixed(mixed):
    if lax.axis_size("hidden") != 2:
        return mixed
    width = mixed.shape[1] // 2
    first = lax.axis_index("hidden") == 0
    low, high = mixed[:, :width], mixed[:, width:]
    moving = swap(jnp.where(first, high, low).astype(jnp.bfloat16))
    return jnp.where(first, low, high) + moving.astype(jnp.float32)


def exchange(block):
    return lax.all_to_all(block, "expert", split_axis=0, concat_axis=0, tiled=True)


def per_device(tokens, gates, routes, w_up, w_down, cotangent):
    expert_count = lax.axis_size("expert")
    tok_rows, top_count = routes.shape
    capacity = 3 * tok_rows * top_count // (2 * expert_count)
    depth = capacity // CHUNKS
    flat_routes = routes.reshape(-1)
    member = (flat_routes[:, None] == jnp.arange(expert_count, dtype=jnp.int32)[None, :]).astype(
        jnp.bfloat16
    )
    order = jnp.arange(tok_rows * top_count, dtype=jnp.int32)
    earlier = (order[:, None] > order[None, :]).astype(jnp.bfloat16)
    before = jnp.dot(earlier, member, preferred_element_type=jnp.float32)
    slot_place = jnp.sum(before * member.astype(jnp.float32), axis=1).astype(jnp.int32)
    slot_chunk = slot_place // depth
    target = (flat_routes * depth + slot_place % depth).reshape(tok_rows, top_count)
    slot_chunk = slot_chunk.reshape(tok_rows, top_count)
    slot_ids = jnp.arange(expert_count * depth, dtype=jnp.int32)

    def selector(chunk, which):
        aim = jnp.where(slot_chunk[:, which] == chunk, target[:, which], -1)
        return (aim[None, :] == slot_ids[:, None]).astype(jnp.bfloat16)

    picks = [[selector(chunk, which) for which in range(top_count)] for chunk in range(CHUNKS)]
    up_local = w_up[0]
    down_local = w_down[0]
    width = cotangent.shape[1]
    own_tokens = lax.dynamic_slice_in_dim(tokens, lax.axis_index("hidden") * width, width, 1)
    cot_float = cotangent.astype(jnp.float32)
    gated = jnp.concatenate(
        [(gates[:, k : k + 1] * cot_float).astype(jnp.bfloat16) for k in range(top_count)], axis=0
    )
    got_tokens = [
        exchange(
            jnp.dot(sum(pick[1:], pick[0]), own_tokens, preferred_element_type=jnp.float32).astype(
                jnp.bfloat16
            )
        )
        for pick in picks
    ]
    got_grads = [
        exchange(
            jnp.dot(
                jnp.concatenate(pick, axis=1), gated, preferred_element_type=jnp.float32
            ).astype(jnp.bfloat16)
        )
        for pick in picks
    ]
    hidden_acts, backs, expert_ins, grad_outs, grad_pres = [], [], [], [], []
    returned, input_back = [], []
    for got in got_tokens:
        expert_in = gather_features(got)
        pre_act = jnp.dot(expert_in, up_local, preferred_element_type=jnp.float32)
        activated, gelu_back = jax.vjp(gelu_fn, pre_act)
        hidden_act = activated.astype(jnp.bfloat16)
        returned.append(exchange(sent_outputs(hidden_act, down_local)))
        expert_ins.append(expert_in)
        hidden_acts.append(hidden_act)
        backs.append(gelu_back)
    for got, gelu_back in zip(got_grads, backs):
        grad_out = gather_features(got)
        grad_hidden = lax.dot_general(
            grad_out, down_local, (((1,), (1,)), ((), ())), preferred_element_type=jnp.float32
        )
        grad_pre = gelu_back(grad_hidden)[0].astype(jnp.bfloat16)
        input_back.append(exchange(summed_features(grad_pre, up_local, 1)))
        grad_outs.append(grad_out)
        grad_pres.append(grad_pre)

    def outer(left, right):
        return lax.dot_general(
            jnp.concatenate(left, axis=0),
            jnp.concatenate(right, axis=0),
            (((0,), (0,)), ((), ())),
            preferred_element_type=jnp.float32,
        ).astype(jnp.bfloat16)

    grad_down = outer(hidden_acts, grad_outs)
    grad_up = outer(expert_ins, grad_pres)

    def picked(chosen, arrays):
        total = None
        for pick, array in zip(chosen, arrays):
            part = lax.dot_general(
                pick, array, (((0,), (0,)), ((), ())), preferred_element_type=jnp.float32
            )
            total = part if total is None else total + part
        return total

    mixed = sum(gates[:, k : k + 1] * picked([pick[k] for pick in picks], returned) for k in range(top_count))
    grad_tokens = picked([sum(pick[1:], pick[0]) for pick in picks], input_back)
    return (
        summed_mixed(mixed).astype(jnp.bfloat16),
        grad_tokens.astype(jnp.bfloat16),
        grad_up[None],
        grad_down[None],
    )


def solution(mesh):
    placed = (
        P("expert", None),
        P("expert", None),
        P("expert", None),
        P("expert", None, "hidden"),
        P("expert", "hidden", None),
        P("expert", "hidden"),
    )
    return jax.shard_map(
        per_device,
        mesh=mesh,
        in_specs=placed,
        out_specs=(
            P("expert", "hidden"),
            P("expert", "hidden"),
            P("expert", None, "hidden"),
            P("expert", "hidden", None),
        ),
        check_vma=False,
    )
```
